32 devices in a mesh: seq: 4 (over x, core), tensor: 8 (over z, y).
Axes of the slice: x: 2, y: 2, z: 4, core: 2. Of those that a mesh axis runs over, the one named last changes fastest.
Arguments:
- hidden: bfloat16 [512, 53248], P('seq', 'tensor'), may hold values from -200 to 200, as said below
- down_int: bfloat16 [53248, 16384], P('tensor', 'seq'), may hold values from -8 to 7, as said below
- w_scale: float32 [16384], P('seq'), may hold values from 0.0004 to 0.0025
- had_small: int32 [52, 52], replicated, may hold values from -1 to 1, as said below
Outputs:
- mixed: bfloat16 [512, 16384], P('tensor', 'seq')
- act_scale: float32 [512], P('seq')
The draws below stay inside these ranges and needn't reach their ends.
Inputs may be any that keep to these rules, and one draw needn't show every extreme that they name: `hidden`: activations with unequal token and channel scales. `down_int`: whole numbers. A Hadamard matrix: entries -1 or +1 and had_small had_small^T = 52 I.
All inputs are finite; a program needn't handle non-finite values.
Results may differ from the reference program's by a relative error of at most 0.0011.
Values may be sent and summed in bfloat16 or wider, within the bound.
A program may use at most 192 MiB of HBM per device.

```python
import math
import jax
import jax.numpy as jnp
import numpy as np
from jax import lax

D = 16384
FF = 53248
HAD = 52
BLOCKS = 1024
TOKENS = 512
N_TENSOR = 8


def draw_hidden(key, part):
    base = jax.random.fold_in(key, 11)
    noise = jnp.clip(jax.random.normal(jax.random.fold_in(base, 1), (TOKENS, FF), jnp.float32), -4.0, 4.0)
    row_scale = jnp.exp(jax.random.uniform(jax.random.fold_in(base, 2), (TOKENS, 1), jnp.float32, jnp.log(0.3), jnp.log(3.0)))
    col_scale = jnp.exp(jax.random.uniform(jax.random.fold_in(base, 3), (1, FF), jnp.float32, jnp.log(0.3), jnp.log(3.0)))
    return (noise * row_scale * col_scale).astype(jnp.bfloat16)


def draw_down_int(key, part):
    values = jax.random.randint(jax.random.fold_in(key, 23), (FF, D), -8, 8, jnp.int32)
    return values.astype(jnp.float32).astype(jnp.bfloat16)


def field_product(left, right):
    left_low, left_high = (left % 5, left // 5)
    right_low, right_high = (right % 5, right // 5)
    low_part = (left_low * right_low + 2 * left_high * right_high) % 5
    high_part = (left_low * right_high + left_high * right_low) % 5
    return low_part + 5 * high_part


def field_difference(left, right):
    return (left % 5 - right % 5) % 5 + 5 * ((left // 5 - right // 5) % 5)


def paley_matrix():
    squares_found = set()
    for element in range(1, 25):
        squares_found.add(field_product(element, element))
    conference = np.zeros((26, 26), np.int64)
    conference[0, 1:] = 1
    conference[1:, 0] = 1
    for row_index in range(25):
        for col_index in range(25):
            gap = field_difference(row_index, col_index)
            if gap == 0:
                conference[row_index + 1, col_index + 1] = 0
            elif gap in squares_found:
                conference[row_index + 1, col_index + 1] = 1
            else:
                conference[row_index + 1, col_index + 1] = -1
    upper_block = np.array([[1, 1], [1, -1]], np.int64)
    lower_block = np.array([[1, -1], [-1, -1]], np.int64)
    return np.kron(conference, upper_block) + np.kron(np.eye(26, dtype=np.int64), lower_block)


def draw_had_small(key, part):
    base_matrix = jnp.asarray(paley_matrix().astype(np.int32))
    row_order = jax.random.permutation(jax.random.fold_in(key, 37), HAD)
    col_order = jax.random.permutation(jax.random.fold_in(key, 41), HAD)
    row_signs = 2 * jax.random.randint(jax.random.fold_in(key, 43), (HAD,), 0, 2, jnp.int32) - 1
    col_signs = 2 * jax.random.randint(jax.random.fold_in(key, 47), (HAD,), 0, 2, jnp.int32) - 1
    permuted = base_matrix[row_order][:, col_order]
    return (row_signs[:, None] * permuted * col_signs[None, :]).astype(jnp.int32)


def block_scale(rng, shape, cuts, least, high):
    level, own = 1.0, jax.random.fold_in(rng, 6)
    for dim, blocks in cuts:
        heights = jnp.exp(jax.random.uniform(jax.random.fold_in(own, dim), (blocks,), jnp.float32, least / len(cuts), high / len(cuts)))
        level = level * jnp.repeat(heights, shape[dim] // blocks).reshape([-1 if axis == dim else 1 for axis in range(len(shape))])
    return level


def setup_inputs(seed: int = 0) -> dict:
    splits = jax.random.split(jax.random.key(seed), 5)
    return {
        "hidden": draw_hidden(jax.random.fold_in(splits[4], 71), 0),
        "down_int": draw_down_int(jax.random.fold_in(splits[4], 71), 0),
        "w_scale": jnp.clip(jnp.exp(math.log(0.0025) - 1.8325815 * jax.random.uniform(splits[2], (D,), jnp.float32) ** block_scale(splits[2], (D,), ((0, 4),), -0.2, 0.2)), 0.0004, 0.0025),
        "had_small": draw_had_small(jax.random.fold_in(splits[4], 71), 0),
    }


clip_ratio = 0.9
epsilon = 1e-05

def sylvester(order):
    left_index = lax.broadcasted_iota(jnp.int32, (order, order), 0)
    right_index = lax.broadcasted_iota(jnp.int32, (order, order), 1)
    both = left_index & right_index
    parity = jnp.zeros((order, order), jnp.int32)
    for shift_bit in range(max(order.bit_length() - 1, 0)):
        parity = parity ^ both >> shift_bit & 1
    return (1 - 2 * parity).astype(jnp.float32)

def reference(hidden, down_int, w_scale, had_small):
    blocked = hidden.astype(jnp.float32).reshape(TOKENS, BLOCKS, HAD)
    first = jnp.einsum('tba,bc->tca', blocked, sylvester(BLOCKS), precision=lax.Precision.HIGHEST)
    second = jnp.einsum('tca,ad->tcd', first, had_small.astype(jnp.float32), precision=lax.Precision.HIGHEST)
    rotated = second.reshape(TOKENS, FF) * jnp.float32(1.0 / math.sqrt(FF))
    peak = lax.optimization_barrier(jnp.max(jnp.abs(rotated), axis=1))
    act_scale = clip_ratio / 7.0 * (peak + epsilon)
    quant = jnp.clip(rotated / act_scale[:, None], -8.0, 7.0)
    width = FF // N_TENSOR

    def accumulate(step, total):
        offset = (step * width).astype(jnp.int32)
        rows_part = lax.dynamic_slice_in_dim(quant, offset, width, 1)
        weight_part = lax.dynamic_slice_in_dim(down_int, offset, width, 0).astype(jnp.float32)
        return total + jnp.dot(rows_part, weight_part, preferred_element_type=jnp.float32, precision=lax.Precision.HIGHEST)
    partial_value = lax.fori_loop(0, N_TENSOR, accumulate, jnp.zeros((TOKENS, D), jnp.float32))
    mixed = (partial_value * act_scale[:, None] * w_scale[None, :]).astype(jnp.bfloat16)
    return (mixed, act_scale)
```

```python
import functools
import math

import jax
import jax.numpy as jnp
from jax import lax
from jax.experimental import pallas as pl
from jax.experimental.pallas import tpu as pltpu
from jax.sharding import PartitionSpec as P

BLOCKS = 1024
LANES = 128
ROWS = 8

clip_ratio = 0.9
epsilon = 1e-05


def parity_sign(left_index, right_index, order):
    both = left_index & right_index
    parity = jnp.zeros(both.shape, jnp.int32)
    for shift_bit in range(max(order.bit_length() - 1, 0)):
        parity = parity ^ ((both >> shift_bit) & 1)
    return 1 - 2 * parity


def inner_factor(had_small, group):
    had = had_small.shape[0]
    width = group * had
    left_index = lax.broadcasted_iota(jnp.int32, (width, had), 0)
    right_index = lax.broadcasted_iota(jnp.int32, (width, had), 1)
    pick = (left_index % had == right_index).astype(jnp.bfloat16)
    tall = jnp.dot(pick, had_small.astype(jnp.bfloat16), preferred_element_type=jnp.float32)
    square = lax.dot_general(
        tall.astype(jnp.bfloat16), pick, (((1,), (1,)), ((), ())), preferred_element_type=jnp.float32
    )
    row_block = lax.broadcasted_iota(jnp.int32, (width, 1), 0) // had
    col_block = lax.broadcasted_iota(jnp.int32, (1, width), 1) // had
    sign = parity_sign(
        jnp.broadcast_to(row_block, (width, width)), jnp.broadcast_to(col_block, (width, width)), group
    )
    return (square * sign.astype(jnp.float32)).astype(jnp.bfloat16)


def rotate_kernel(count, rows, norm_factor, x_ref, k_ref, *rest):
    out_refs, scale_ref, y_ref = rest[:-2], rest[-2], rest[-1]
    width = k_ref.shape[0]
    inner = x_ref.shape[1] // width
    chunks = count * inner
    lane_tiles = width // LANES
    for j in range(inner):
        y_ref[j] = jnp.dot(
            x_ref[:, j * width : (j + 1) * width], k_ref[...], preferred_element_type=jnp.float32
        )
    for h, out_ref in enumerate(out_refs):
        def mix(tile, peak):
            cols = pl.ds(pl.multiple_of(tile * LANES, LANES), LANES)
            vals = [
                y_ref[c % inner, pl.ds((c // inner) * rows + h * ROWS, ROWS), cols] for c in range(chunks)
            ]
            span = 1
            while span < chunks:
                for c in range(chunks):
                    if c & span == 0:
                        vals[c], vals[c + span] = vals[c] + vals[c + span], vals[c] - vals[c + span]
                span *= 2
            for c in range(chunks):
                rotated = vals[c] * norm_factor
                peak = jnp.maximum(peak, jnp.abs(rotated))
                y_ref[c % inner, pl.ds((c // inner) * rows + h * ROWS, ROWS), cols] = rotated
            return peak

        peak = lax.fori_loop(0, lane_tiles, mix, jnp.zeros((ROWS, LANES), jnp.float32))
        peak = jnp.max(peak, axis=1, keepdims=True)
        scale = jnp.broadcast_to(clip_ratio / 7.0 * (peak + epsilon), (ROWS, LANES))
        scale_ref[pl.ds(h * ROWS, ROWS), :] = scale

        def split(tile, carry):
            cols = pl.ds(pl.multiple_of(tile * LANES, LANES), LANES)
            for c in range(chunks):
                rotated = y_ref[c % inner, pl.ds((c // inner) * rows + h * ROWS, ROWS), cols]
                quant = jnp.clip(rotated / scale, -8.0, 7.0)
                high = quant.astype(jnp.bfloat16).astype(jnp.float32)
                both = jnp.concatenate([high, quant - high], axis=0).astype(jnp.bfloat16)
                place = pl.ds(pl.multiple_of((c % inner) * width + tile * LANES, LANES), LANES)
                out_ref[pl.ds((c // inner) * 2 * ROWS, 2 * ROWS), place] = both
            return carry

        lax.fori_loop(0, lane_tiles, split, 0)


def local(hidden, down_int, w_scale, had_small):
    tensor_count = lax.axis_size("tensor")
    seq_count = lax.axis_size("seq")
    tokens_here, units_here = hidden.shape
    had = had_small.shape[0]
    units = units_here * tensor_count
    rows = tokens_here // tensor_count
    parts = rows // ROWS
    group = LANES // math.gcd(had, LANES)
    width = group * had
    inner = units_here // width
    norm_factor = 1.0 / math.sqrt(units)

    factor = inner_factor(had_small, group)
    gathered = lax.all_to_all(
        hidden.reshape(tensor_count, rows, units_here), "tensor", split_axis=0, concat_axis=0, tiled=True
    ).reshape(tokens_here, units_here)
    *quants, scales = pl.pallas_call(
        functools.partial(rotate_kernel, tensor_count, rows, norm_factor),
        out_shape=[jax.ShapeDtypeStruct((tensor_count * 2 * ROWS, units_here), jnp.bfloat16)] * parts
        + [jax.ShapeDtypeStruct((rows, LANES), jnp.float32)],
        in_specs=[pl.BlockSpec(memory_space=pltpu.VMEM)] * 2,
        out_specs=[pl.BlockSpec(memory_space=pltpu.VMEM)] * (parts + 1),
        scratch_shapes=[pltpu.VMEM((inner, tokens_here, width), jnp.float32)],
        compiler_params=pltpu.CompilerParams(vmem_limit_bytes=40 * 1024 * 1024),
        cost_estimate=pl.CostEstimate(
            flops=2 * inner * tokens_here * width * width,
            bytes_accessed=6 * tokens_here * units_here + 2 * width * width,
            transcendentals=0,
        ),
        name="rotate",
    )(gathered, factor)

    all_scale = lax.all_gather(scales, ("seq", "tensor"), axis=0, tiled=True)[:, 0]
    total_tokens = tokens_here * seq_count
    own_rows = total_tokens // tensor_count
    summed = []
    for quant in quants:
        returned = lax.all_to_all(
            quant.reshape(tensor_count, 2 * ROWS, units_here), "tensor", split_axis=0, concat_axis=0, tiled=True
        ).reshape(tensor_count * 2 * ROWS, units_here)
        all_quant = lax.all_gather(returned, "seq", axis=0, tiled=True)
        terms = jnp.dot(all_quant, down_int, preferred_element_type=jnp.float32)
        terms = terms.reshape(seq_count * tensor_count, 2, ROWS, -1)
        partial_value = (terms[:, 0] + terms[:, 1]).reshape(total_tokens // parts, -1)
        summed.append(lax.psum_scatter(partial_value, "tensor", scatter_dimension=0, tiled=True))
    row_scale = lax.dynamic_slice_in_dim(all_scale, lax.axis_index("tensor") * own_rows, own_rows, 0)
    act_scale = lax.dynamic_slice_in_dim(all_scale, lax.axis_index("seq") * tokens_here, tokens_here, 0)
    tiles = own_rows // rows
    stacked = jnp.stack([part.reshape(tiles, ROWS, -1) for part in summed], axis=1).reshape(own_rows, -1)
    mixed = (stacked * row_scale[:, None] * w_scale[None, :]).astype(jnp.bfloat16)
    return (mixed, act_scale)


def solution(mesh):
    return jax.shard_map(
        local,
        mesh=mesh,
        in_specs=(P("seq", "tensor"), P("tensor", "seq"), P("seq"), P()),
        out_specs=(P("tensor", "seq"), P("seq")),
        check_vma=False,
    )
```

```python
import functools
import math

import jax
import jax.numpy as jnp
from jax import lax
from jax.experimental import pallas as pl
from jax.experimental.pallas import tpu as pltpu
from jax.sharding import PartitionSpec as P

BLOCKS = 1024
LANES = 128
ROWS = 8
LAG = 3

clip_ratio = 0.9
epsilon = 1e-05


def parity_sign(left_index, right_index, order):
    both = left_index & right_index
    parity = jnp.zeros(both.shape, jnp.int32)
    for shift_bit in range(max(order.bit_length() - 1, 0)):
        parity = parity ^ ((both >> shift_bit) & 1)
    return 1 - 2 * parity


def inner_factor(had_small, group):
    had = had_small.shape[0]
    width = group * had
    left_index = lax.broadcasted_iota(jnp.int32, (width, had), 0)
    right_index = lax.broadcasted_iota(jnp.int32, (width, had), 1)
    pick = (left_index % had == right_index).astype(jnp.bfloat16)
    tall = jnp.dot(pick, had_small.astype(jnp.bfloat16), preferred_element_type=jnp.float32)
    square = lax.dot_general(
        tall.astype(jnp.bfloat16), pick, (((1,), (1,)), ((), ())), preferred_element_type=jnp.float32
    )
    row_block = lax.broadcasted_iota(jnp.int32, (width, 1), 0) // had
    col_block = lax.broadcasted_iota(jnp.int32, (1, width), 1) // had
    sign = parity_sign(
        jnp.broadcast_to(row_block, (width, width)), jnp.broadcast_to(col_block, (width, width)), group
    )
    return (square * sign.astype(jnp.float32)).astype(jnp.bfloat16)


def rotate_kernel(count, rows, norm_factor, x_ref, k_ref, *rest):
    out_refs, y_ref = rest[:-1], rest[-1]
    width = k_ref.shape[0]
    inner = x_ref.shape[1] // width
    chunks = count * inner
    lane_tiles = width // LANES
    for j in range(inner):
        y_ref[j] = jnp.dot(
            x_ref[:, j * width : (j + 1) * width], k_ref[...], preferred_element_type=jnp.float32
        )
    for h, out_ref in enumerate(out_refs):
        def mix(tile, peak):
            cols = pl.ds(pl.multiple_of(tile * LANES, LANES), LANES)
            vals = [
                y_ref[c % inner, pl.ds((c // inner) * rows + h * ROWS, ROWS), cols] for c in range(chunks)
            ]
            span = 1
            while span < chunks:
                for c in range(chunks):
                    if c & span == 0:
                        vals[c], vals[c + span] = vals[c] + vals[c + span], vals[c] - vals[c + span]
                span *= 2
            for c in range(chunks):
                rotated = vals[c] * norm_factor
                peak = jnp.maximum(peak, jnp.abs(rotated))
                y_ref[c % inner, pl.ds((c // inner) * rows + h * ROWS, ROWS), cols] = rotated
            return peak

        peak = lax.fori_loop(0, lane_tiles, mix, jnp.zeros((ROWS, LANES), jnp.float32))
        peak = jnp.max(peak, axis=1, keepdims=True)
        scale = jnp.broadcast_to(clip_ratio / 7.0 * (peak + epsilon), (ROWS, LANES))
        top = scale.astype(jnp.bfloat16).astype(jnp.float32)
        middle = (scale - top).astype(jnp.bfloat16).astype(jnp.float32)
        lane = lax.broadcasted_iota(jnp.int32, (ROWS, LANES), 1)
        first = jnp.where(lane < LANES // 2, top, scale - top - middle)
        terms = jnp.concatenate([first, middle], axis=0).astype(jnp.bfloat16)
        for i in range(count):
            out_ref[pl.ds(i * 2 * ROWS, 2 * ROWS), pl.ds(inner * width, LANES)] = terms

        def split(tile, carry):
            cols = pl.ds(pl.multiple_of(tile * LANES, LANES), LANES)
            for c in range(chunks):
                rotated = y_ref[c % inner, pl.ds((c // inner) * rows + h * ROWS, ROWS), cols]
                quant = jnp.clip(rotated / scale, -8.0, 7.0)
                high = quant.astype(jnp.bfloat16).astype(jnp.float32)
                both = jnp.concatenate([high, quant - high], axis=0).astype(jnp.bfloat16)
                place = pl.ds(pl.multiple_of((c % inner) * width + tile * LANES, LANES), LANES)
                out_ref[pl.ds((c // inner) * 2 * ROWS, 2 * ROWS), place] = both
            return carry

        lax.fori_loop(0, lane_tiles, split, 0)


def product_kernel(tiles, x_ref, w_ref, gain_ref, out_ref, scale_ref, mine, half, from_pair, from_line, *sems):
    pair_send, pair_recv, line_send, line_recv = sems
    step = pl.program_id(0)
    me = lax.axis_index("tensor")
    parity = me % 2
    place = me // 2
    line = mine.shape[2]
    own = mine.shape[3]
    span = w_ref.shape[1]
    narrow = min(256, span)
    depth = w_ref.shape[0]
    partner = me + 1 - 2 * parity

    def pair_copy(tile):
        return pltpu.make_async_remote_copy(
            src_ref=mine.at[tile, 1 - parity],
            dst_ref=from_pair.at[tile],
            send_sem=pair_send.at[tile],
            recv_sem=pair_recv.at[tile],
            device_id={"tensor": partner},
            device_id_type=pl.DeviceIdType.MESH,
        )

    def line_copy(tile, hop):
        target = (place + hop) % line
        return pltpu.make_async_remote_copy(
            src_ref=half.at[tile, target],
            dst_ref=from_line.at[tile, hop - 1],
            send_sem=line_send.at[tile, hop - 1],
            recv_sem=line_recv.at[tile, hop - 1],
            device_id={"tensor": 2 * target + parity},
            device_id_type=pl.DeviceIdType.MESH,
        )

    @pl.when(step == 0)
    def _():
        barrier = pltpu.get_barrier_semaphore()
        pl.semaphore_signal(
            barrier, inc=1, device_id={"tensor": partner}, device_id_type=pl.DeviceIdType.MESH
        )
        for hop in range(1, line):
            pl.semaphore_signal(
                barrier,
                inc=1,
                device_id={"tensor": 2 * ((place + hop) % line) + parity},
                device_id_type=pl.DeviceIdType.MESH,
            )
        pl.semaphore_wait(barrier, line)
        terms = x_ref[:, depth:].astype(jnp.float32).reshape(-1, 2, ROWS, LANES)
        first = terms[:, 0].reshape(-1, LANES)
        middle = terms[:, 1].reshape(-1, LANES)
        scale_ref[...] = first + middle + pltpu.roll(first, LANES // 2, 1)

    @pl.when(step < tiles)
    def _():
        def piece(n, carry):
            cols = pl.ds(pl.multiple_of(n * narrow, narrow), narrow)
            terms = jnp.dot(x_ref[:, :depth], w_ref[:, cols], preferred_element_type=jnp.float32)
            terms = terms.reshape(-1, 2, ROWS, narrow)
            sums = (terms[:, 0] + terms[:, 1]).reshape(2 * line, own, narrow)
            for owner in range(2 * line):
                mine[step, owner % 2, owner // 2, :, cols] = sums[owner]
            return carry

        lax.fori_loop(0, span // narrow, piece, 0)
        pair_copy(step).start()

    @pl.when((step >= 1) & (step <= tiles))
    def _():
        tile = step - 1
        pair_copy(tile).wait_recv()
        half[tile] = mine[tile, parity] + from_pair[tile]
        for hop in range(1, line):
            line_copy(tile, hop).start()

    @pl.when(step >= LAG)
    def _():
        tile = step - LAG
        total = half[tile, place]
        for hop in range(1, line):
            line_copy(tile, hop).wait_recv()
            total = total + from_line[tile, hop - 1]
        cols = pl.ds(pl.multiple_of(tile * span, span), span)
        scale = scale_ref[pl.ds(pl.multiple_of(me * own, own), own), :][:, :1]
        out_ref[:, cols] = total * scale * gain_ref[:, cols]
        pair_copy(tile).wait_send()
        for hop in range(1, line):
            line_copy(tile, hop).wait_send()


def product_and_sum(all_quant, down_int, gain, tensor_count, tokens):
    depth, columns = down_int.shape
    span = min(512, columns)
    tiles = columns // span
    line = tensor_count // 2
    own = tokens // tensor_count
    return pl.pallas_call(
        functools.partial(product_kernel, tiles),
        grid=(tiles + LAG,),
        out_shape=[
            jax.ShapeDtypeStruct((own, columns), jnp.float32),
            jax.ShapeDtypeStruct((tokens, LANES), jnp.float32),
        ],
        in_specs=[
            pl.BlockSpec(memory_space=pltpu.VMEM),
            pl.BlockSpec((depth, span), lambda i: (0, jnp.minimum(i, tiles - 1))),
            pl.BlockSpec(memory_space=pltpu.VMEM),
        ],
        out_specs=[pl.BlockSpec(memory_space=pltpu.VMEM)] * 2,
        scratch_shapes=[
            pltpu.VMEM((tiles, 2, line, own, span), jnp.float32),
            pltpu.VMEM((tiles, line, own, span), jnp.float32),
            pltpu.VMEM((tiles, line, own, span), jnp.float32),
            pltpu.VMEM((tiles, line - 1, own, span), jnp.float32),
            pltpu.SemaphoreType.DMA((tiles,)),
            pltpu.SemaphoreType.DMA((tiles,)),
            pltpu.SemaphoreType.DMA((tiles, line - 1)),
            pltpu.SemaphoreType.DMA((tiles, line - 1)),
        ],
        compiler_params=pltpu.CompilerParams(
            collective_id=0, has_side_effects=True, vmem_limit_bytes=60 * 1024 * 1024
        ),
        cost_estimate=pl.CostEstimate(
            flops=4 * tokens * depth * columns, bytes_accessed=2 * depth * columns, transcendentals=0
        ),
        name="product_and_sum",
    )(all_quant, down_int, gain)


def local(hidden, down_int, w_scale, had_small):
    tensor_count = lax.axis_size("tensor")
    seq_count = lax.axis_size("seq")
    tokens_here, units_here = hidden.shape
    had = had_small.shape[0]
    units = units_here * tensor_count
    rows = tokens_here // tensor_count
    parts = rows // ROWS
    group = LANES // math.gcd(had, LANES)
    width = group * had
    inner = units_here // width
    norm_factor = 1.0 / math.sqrt(units)

    factor = inner_factor(had_small, group)
    gathered = lax.all_to_all(
        hidden.reshape(tensor_count, rows, units_here), "tensor", split_axis=0, concat_axis=0, tiled=True
    ).reshape(tokens_here, units_here)
    quants = pl.pallas_call(
        functools.partial(rotate_kernel, tensor_count, rows, norm_factor),
        out_shape=[jax.ShapeDtypeStruct((tensor_count * 2 * ROWS, units_here + LANES), jnp.bfloat16)] * parts,
        in_specs=[pl.BlockSpec(memory_space=pltpu.VMEM)] * 2,
        out_specs=[pl.BlockSpec(memory_space=pltpu.VMEM)] * parts,
        scratch_shapes=[pltpu.VMEM((inner, tokens_here, width), jnp.float32)],
        compiler_params=pltpu.CompilerParams(vmem_limit_bytes=40 * 1024 * 1024),
        cost_estimate=pl.CostEstimate(
            flops=2 * inner * tokens_here * width * width,
            bytes_accessed=6 * tokens_here * units_here + 2 * width * width,
            transcendentals=0,
        ),
        name="rotate",
    )(gathered, factor)

    total_tokens = tokens_here * seq_count
    own_rows = total_tokens // tensor_count
    outs, scales = [], []
    for quant in quants:
        returned = lax.all_to_all(
            quant.reshape(tensor_count, 2 * ROWS, -1), "tensor", split_axis=0, concat_axis=0, tiled=True
        ).reshape(tensor_count * 2 * ROWS, -1)
        all_quant = lax.all_gather(returned, "seq", axis=0, tiled=True)
        summed, scale = product_and_sum(
            all_quant, down_int, w_scale[None, :], tensor_count, total_tokens // parts
        )
        outs.append(summed.reshape(own_rows // rows, ROWS, -1))
        offset = lax.axis_index("seq") * (tokens_here // parts)
        here = lax.dynamic_slice_in_dim(scale, offset, tokens_here // parts, 0)
        scales.append(here.reshape(tensor_count, ROWS, LANES))
    mixed = jnp.stack(outs, axis=1).reshape(own_rows, -1).astype(jnp.bfloat16)
    act_scale = jnp.stack(scales, axis=1).reshape(tokens_here, LANES)[:, 0]
    return (mixed, act_scale)


def solution(mesh):
    return jax.shard_map(
        local,
        mesh=mesh,
        in_specs=(P("seq", "tensor"), P("tensor", "seq"), P("seq"), P()),
        out_specs=(P("tensor", "seq"), P("seq")),
        check_vma=False,
    )
```

```python
import functools
import math

import jax
import jax.numpy as jnp
from jax import lax
from jax.experimental import pallas as pl
from jax.experimental.pallas import tpu as pltpu
from jax.sharding import PartitionSpec as P

BLOCKS = 1024
LANES = 128
ROWS = 8
LAG = 3

clip_ratio = 0.9
epsilon = 1e-05


def parity_sign(left_index, right_index, order):
    both = left_index & right_index
    parity = jnp.zeros(both.shape, jnp.int32)
    for shift_bit in range(max(order.bit_length() - 1, 0)):
        parity = parity ^ ((both >> shift_bit) & 1)
    return 1 - 2 * parity


def inner_factor(had_small, group):
    had = had_small.shape[0]
    width = group * had
    left_index = lax.broadcasted_iota(jnp.int32, (width, had), 0)
    right_index = lax.broadcasted_iota(jnp.int32, (width, had), 1)
    pick = (left_index % had == right_index).astype(jnp.bfloat16)
    tall = jnp.dot(pick, had_small.astype(jnp.bfloat16), preferred_element_type=jnp.float32)
    square = lax.dot_general(
        tall.astype(jnp.bfloat16), pick, (((1,), (1,)), ((), ())), preferred_element_type=jnp.float32
    )
    row_block = lax.broadcasted_iota(jnp.int32, (width, 1), 0) // had
    col_block = lax.broadcasted_iota(jnp.int32, (1, width), 1) // had
    sign = parity_sign(
        jnp.broadcast_to(row_block, (width, width)), jnp.broadcast_to(col_block, (width, width)), group
    )
    return (square * sign.astype(jnp.float32)).astype(jnp.bfloat16)


def rotate_kernel(count, rows, norm_factor, x_ref, k_ref, *rest):
    out_refs, y_ref = rest[:-1], rest[-1]
    width = k_ref.shape[0]
    inner = x_ref.shape[1] // width
    chunks = count * inner
    lane_tiles = width // LANES
    for j in range(inner):
        y_ref[j] = jnp.dot(
            x_ref[:, j * width : (j + 1) * width], k_ref[...], preferred_element_type=jnp.float32
        )
    for h, out_ref in enumerate(out_refs):
        def mix(tile, peak):
            cols = pl.ds(pl.multiple_of(tile * LANES, LANES), LANES)
            vals = [
                y_ref[c % inner, pl.ds((c // inner) * rows + h * ROWS, ROWS), cols] for c in range(chunks)
            ]
            span = 1
            while span < chunks:
                for c in range(chunks):
                    if c & span == 0:
                        vals[c], vals[c + span] = vals[c] + vals[c + span], vals[c] - vals[c + span]
                span *= 2
            for c in range(chunks):
                rotated = vals[c] * norm_factor
                peak = jnp.maximum(peak, jnp.abs(rotated))
                y_ref[c % inner, pl.ds((c // inner) * rows + h * ROWS, ROWS), cols] = rotated
            return peak

        peak = lax.fori_loop(0, lane_tiles, mix, jnp.zeros((ROWS, LANES), jnp.float32))
        peak = jnp.max(peak, axis=1, keepdims=True)
        scale = jnp.broadcast_to(clip_ratio / 7.0 * (peak + epsilon), (ROWS, LANES))
        top = scale.astype(jnp.bfloat16).astype(jnp.float32)
        middle = (scale - top).astype(jnp.bfloat16).astype(jnp.float32)
        lane = lax.broadcasted_iota(jnp.int32, (ROWS, LANES), 1)
        first = jnp.where(lane < LANES // 2, top, scale - top - middle)
        terms = jnp.concatenate([first, middle], axis=0).astype(jnp.bfloat16)
        for i in range(count):
            out_ref[pl.ds(i * 2 * ROWS, 2 * ROWS), pl.ds(inner * width, LANES)] = terms

        def split(tile, carry):
            cols = pl.ds(pl.multiple_of(tile * LANES, LANES), LANES)
            for c in range(chunks):
                rotated = y_ref[c % inner, pl.ds((c // inner) * rows + h * ROWS, ROWS), cols]
                quant = jnp.clip(rotated / scale, -8.0, 7.0)
                high = quant.astype(jnp.bfloat16).astype(jnp.float32)
                both = jnp.concatenate([high, quant - high], axis=0).astype(jnp.bfloat16)
                place = pl.ds(pl.multiple_of((c % inner) * width + tile * LANES, LANES), LANES)
                out_ref[pl.ds((c // inner) * 2 * ROWS, 2 * ROWS), place] = both
            return carry

        lax.fori_loop(0, lane_tiles, split, 0)


def product_kernel(tiles, x_ref, w_ref, gain_ref, out_ref, scale_ref, mine, half, from_pair, from_line, *sems):
    pair_send, pair_recv, line_send, line_recv = sems
    step = pl.program_id(0)
    me = lax.axis_index("tensor")
    parity = me % 2
    place = me // 2
    line = mine.shape[2]
    own = mine.shape[3]
    span = w_ref.shape[1]
    narrow = min(256, span)
    depth = w_ref.shape[0]
    partner = me + 1 - 2 * parity

    def pair_copy(tile):
        return pltpu.make_async_remote_copy(
            src_ref=mine.at[tile, 1 - parity],
            dst_ref=from_pair.at[tile],
            send_sem=pair_send.at[tile],
            recv_sem=pair_recv.at[tile],
            device_id={"tensor": partner},
            device_id_type=pl.DeviceIdType.MESH,
        )

    def line_copy(tile, hop):
        target = (place + hop) % line
        return pltpu.make_async_remote_copy(
            src_ref=half.at[tile, target],
            dst_ref=from_line.at[tile, hop - 1],
            send_sem=line_send.at[tile, hop - 1],
            recv_sem=line_recv.at[tile, hop - 1],
            device_id={"tensor": 2 * target + parity},
            device_id_type=pl.DeviceIdType.MESH,
        )

    @pl.when(step == 0)
    def _():
        barrier = pltpu.get_barrier_semaphore()
        pl.semaphore_signal(
            barrier, inc=1, device_id={"tensor": partner}, device_id_type=pl.DeviceIdType.MESH
        )
        for hop in range(1, line):
            pl.semaphore_signal(
                barrier,
                inc=1,
                device_id={"tensor": 2 * ((place + hop) % line) + parity},
                device_id_type=pl.DeviceIdType.MESH,
            )
        pl.semaphore_wait(barrier, line)
        terms = x_ref[:, depth:].astype(jnp.float32).reshape(-1, 2, ROWS, LANES)
        first = terms[:, 0].reshape(-1, LANES)
        middle = terms[:, 1].reshape(-1, LANES)
        scale_ref[...] = first + middle + pltpu.roll(first, LANES // 2, 1)

    @pl.when(step < tiles)
    def _():
        def piece(n, carry):
            cols = pl.ds(pl.multiple_of(n * narrow, narrow), narrow)
            terms = jnp.dot(x_ref[:, :depth], w_ref[:, cols], preferred_element_type=jnp.float32)
            terms = terms.reshape(-1, 2, ROWS, narrow)
            sums = (terms[:, 0] + terms[:, 1]).reshape(2 * line, own, narrow)
            for owner in range(2 * line):
                mine[step, owner % 2, owner // 2, :, cols] = sums[owner]
            return carry

        lax.fori_loop(0, span // narrow, piece, 0)
        pair_copy(step).start()

    @pl.when((step >= 1) & (step <= tiles))
    def _():
        tile = step - 1
        pair_copy(tile).wait_recv()
        half[tile] = mine[tile, parity] + from_pair[tile]
        for hop in range(1, line):
            line_copy(tile, hop).start()

    @pl.when(step >= LAG)
    def _():
        tile = step - LAG
        total = half[tile, place]
        for hop in range(1, line):
            line_copy(tile, hop).wait_recv()
            total = total + from_line[tile, hop - 1]
        cols = pl.ds(pl.multiple_of(tile * span, span), span)
        scale = scale_ref[pl.ds(pl.multiple_of(me * own, own), own), :][:, :1]
        out_ref[:, cols] = total * scale * gain_ref[:, cols]
        pair_copy(tile).wait_send()
        for hop in range(1, line):
            line_copy(tile, hop).wait_send()


def product_and_sum(all_quant, down_int, gain, tensor_count, tokens):
    depth, columns = down_int.shape
    span = min(256, columns)
    tiles = columns // span
    line = tensor_count // 2
    own = tokens // tensor_count
    return pl.pallas_call(
        functools.partial(product_kernel, tiles),
        grid=(tiles + LAG,),
        out_shape=[
            jax.ShapeDtypeStruct((own, columns), jnp.float32),
            jax.ShapeDtypeStruct((tokens, LANES), jnp.float32),
        ],
        in_specs=[
            pl.BlockSpec(memory_space=pltpu.VMEM),
            pl.BlockSpec((depth, span), lambda i: (0, jnp.minimum(i, tiles - 1))),
            pl.BlockSpec(memory_space=pltpu.VMEM),
        ],
        out_specs=[pl.BlockSpec(memory_space=pltpu.VMEM)] * 2,
        scratch_shapes=[
            pltpu.VMEM((tiles, 2, line, own, span), jnp.float32),
            pltpu.VMEM((tiles, line, own, span), jnp.float32),
            pltpu.VMEM((tiles, line, own, span), jnp.float32),
            pltpu.VMEM((tiles, line - 1, own, span), jnp.float32),
            pltpu.SemaphoreType.DMA((tiles,)),
            pltpu.SemaphoreType.DMA((tiles,)),
            pltpu.SemaphoreType.DMA((tiles, line - 1)),
            pltpu.SemaphoreType.DMA((tiles, line - 1)),
        ],
        compiler_params=pltpu.CompilerParams(
            collective_id=0, has_side_effects=True, vmem_limit_bytes=60 * 1024 * 1024
        ),
        cost_estimate=pl.CostEstimate(
            flops=4 * tokens * depth * columns, bytes_accessed=2 * depth * columns, transcendentals=0
        ),
        name="product_and_sum",
    )(all_quant, down_int, gain)


def local(hidden, down_int, w_scale, had_small):
    tensor_count = lax.axis_size("tensor")
    seq_count = lax.axis_size("seq")
    tokens_here, units_here = hidden.shape
    had = had_small.shape[0]
    units = units_here * tensor_count
    rows = tokens_here // tensor_count
    parts = rows // ROWS
    group = LANES // math.gcd(had, LANES)
    width = group * had
    inner = units_here // width
    norm_factor = 1.0 / math.sqrt(units)

    factor = inner_factor(had_small, group)
    gathered = lax.all_to_all(
        hidden.reshape(tensor_count, rows, units_here), "tensor", split_axis=0, concat_axis=0, tiled=True
    ).reshape(tokens_here, units_here)
    quants = pl.pallas_call(
        functools.partial(rotate_kernel, tensor_count, rows, norm_factor),
        out_shape=[jax.ShapeDtypeStruct((tensor_count * 2 * ROWS, units_here + LANES), jnp.bfloat16)] * parts,
        in_specs=[pl.BlockSpec(memory_space=pltpu.VMEM)] * 2,
        out_specs=[pl.BlockSpec(memory_space=pltpu.VMEM)] * parts,
        scratch_shapes=[pltpu.VMEM((inner, tokens_here, width), jnp.float32)],
        compiler_params=pltpu.CompilerParams(vmem_limit_bytes=40 * 1024 * 1024),
        cost_estimate=pl.CostEstimate(
            flops=2 * inner * tokens_here * width * width,
            bytes_accessed=6 * tokens_here * units_here + 2 * width * width,
            transcendentals=0,
        ),
        name="rotate",
    )(gathered, factor)

    total_tokens = tokens_here * seq_count
    own_rows = total_tokens // tensor_count
    outs, scales = [], []
    for quant in quants:
        returned = lax.all_to_all(
            quant.reshape(tensor_count, 2 * ROWS, -1), "tensor", split_axis=0, concat_axis=0, tiled=True
        ).reshape(tensor_count * 2 * ROWS, -1)
        all_quant = lax.all_gather(returned, "seq", axis=0, tiled=True)
        summed, scale = product_and_sum(
            all_quant, down_int, w_scale[None, :], tensor_count, total_tokens // parts
        )
        outs.append(summed.reshape(own_rows // rows, ROWS, -1))
        offset = lax.axis_index("seq") * (tokens_here // parts)
        here = lax.dynamic_slice_in_dim(scale, offset, tokens_here // parts, 0)
        scales.append(here.reshape(tensor_count, ROWS, LANES))
    mixed = jnp.stack(outs, axis=1).reshape(own_rows, -1).astype(jnp.bfloat16)
    act_scale = jnp.stack(scales, axis=1).reshape(tokens_here, LANES)[:, 0]
    return (mixed, act_scale)


def solution(mesh):
    return jax.shard_map(
        local,
        mesh=mesh,
        in_specs=(P("seq", "tensor"), P("tensor", "seq"), P("seq"), P()),
        out_specs=(P("tensor", "seq"), P("seq")),
        check_vma=False,
    )
```
